32 devices in a mesh: grp: 2 (over y), row: 8 (over z, x), ch: 1, sub: 2 (over core).
Axes of the slice: x: 2, y: 2, z: 4, core: 2. Of those that a mesh axis runs over, the one named last changes fastest.
Arguments:
- pair_field: bfloat16 [128, 256, 128], P(None, ('grp', 'row', 'sub'), 'ch'), parts along dimension 1, may hold values from -6 to 6
- residue_mask: int32 [256], P('grp'), parts along dimension 0, may hold values from 0 to 1, as said below
- input_gain: float32 [2, 128], replicated, may hold values from 0.1 to 1.9
- projection_weight: bfloat16 [2, 128, 512], replicated, may hold values from -0.5 to 0.5
- gate_weight: bfloat16 [2, 128, 128], replicated, may hold values from -0.5 to 0.5
- output_gain: float32 [2, 128], replicated, may hold values from 0.1 to 1.9
- output_weight: bfloat16 [2, 128, 128], replicated, may hold values from -0.5 to 0.5
Outputs:
- updated_pair: bfloat16 [128, 256, 128], P(None, ('grp', 'row', 'sub'), 'ch'), parts along dimension 1
The draws below stay inside these ranges and needn't reach their ends.
There are 2 independent parts, one for each index of `grp`. The reference program is written for one: setup_inputs(seed, part) draws one part's arguments, and reference() takes and returns one part's arrays. A program takes and returns all parts, laid end to end along the dimension named above; an argument that names none is the same for every part. Nothing has to cross between parts.
Inputs may be any that keep to these rules, and one draw needn't show every extreme that they name: `residue_mask`: ones at positions 0 up to some count and zeros after it; at least 64 ones and at least one zero.
All inputs are finite; a program needn't handle non-finite values.
Results may differ from the reference program's by a relative error of at most 0.015.
Values may be sent and summed in bfloat16 or wider, within the bound.
A program may use at most 64 MiB of HBM per device.

```python
import math
import jax
import jax.numpy as jnp
from jax import lax

C = 128
C_HID = 128
N = 128


def draw_residue_mask(key, part):
    key = jax.random.fold_in(key, 7)
    kept_count = jax.random.randint(key, (), N // 2, N)
    return (jnp.arange(N) < kept_count).astype(jnp.int32)


def block_levels(rng, dims, shards, smallest, top_value):
    level, own = 1.0, jax.random.fold_in(rng, 6)
    for dim, parts in shards:
        heights = jnp.exp(jax.random.uniform(jax.random.fold_in(own, dim), (parts,), jnp.float32, smallest / len(shards), top_value / len(shards)))
        level = level * jnp.repeat(heights, dims[dim] // parts).reshape([-1 if axis == dim else 1 for axis in range(len(dims))])
    return level


def normal_values(key, dims, deviation, reach, pieces=(), kind=jnp.bfloat16):
    result = jax.random.normal(key, dims, jnp.float32) * deviation
    if len(pieces) > 0:
        result = block_levels(key, dims, pieces, -0.22, 0.18) * result
    return jnp.clip(result, min=-reach, max=reach).astype(kind)


def setup_inputs(seed: int = 0, part: int = 0) -> dict:
    arg_keys = jax.random.split(jax.random.key(seed), 8)
    part_keys = jax.random.split(jax.random.fold_in(arg_keys[7], part), 8)
    return {
        "pair_field": normal_values(part_keys[0], (C, N, N), 1.0, 6.0, ((1, 16),)),
        "residue_mask": draw_residue_mask(jax.random.fold_in(jax.random.fold_in(arg_keys[7], part), 71), part),
        "input_gain": jnp.clip(1.0 + 0.18 * jax.random.normal(arg_keys[2], (2, C), jnp.float32), 0.1, 1.9),
        "projection_weight": normal_values(arg_keys[3], (2, C, 4 * C_HID), C ** -0.5, 0.5),
        "gate_weight": normal_values(arg_keys[4], (2, C, C), C ** -0.5, 0.5),
        "output_gain": jnp.clip(1.0 + 0.18 * jax.random.normal(arg_keys[5], (2, C_HID), jnp.float32), 0.1, 1.9),
        "output_weight": normal_values(arg_keys[6], (2, C_HID, C), C_HID ** -0.5, 0.5),
    }


EPS = 1e-05

def channel_norm(values, gain_vector):
    average = lax.optimization_barrier(jnp.mean(values, axis=0, keepdims=True))
    centred = values - average
    spread = lax.optimization_barrier(jnp.mean(centred * centred, axis=0, keepdims=True))
    return centred * lax.rsqrt(spread + EPS) * gain_vector[:, None, None]

def reference(pair_field, residue_mask, input_gain, projection_weight, gate_weight, output_gain, output_weight):
    channels = pair_field.shape[0]
    length = pair_field.shape[1]
    hidden = output_weight.shape[1]
    row_block = math.gcd(length, 64)
    blocks_count = length // row_block
    mask_float = residue_mask.astype(jnp.float32)
    mask_blocks = mask_float.reshape(blocks_count, row_block)

    def split_rows(values):
        return values.reshape(values.shape[0], blocks_count, row_block, length).transpose(1, 0, 2, 3)

    def join_rows(values):
        return values.transpose(1, 0, 2, 3).reshape(values.shape[1], length, length)
    current = pair_field
    for update in range(2):

        def project_rows(operands):
            rows_slab, mask_rows = operands
            normed = channel_norm(rows_slab.astype(jnp.float32), input_gain[update]).astype(jnp.bfloat16)
            projected = jnp.einsum('dpq,de->epq', normed.astype(jnp.float32), projection_weight[update].astype(jnp.float32))
            pair_mask = mask_rows[:, None] * mask_float[None, :]
            left_proj = (pair_mask * jax.nn.sigmoid(projected[hidden:2 * hidden]) * projected[:hidden]).astype(jnp.bfloat16)
            right_proj = (pair_mask * jax.nn.sigmoid(projected[3 * hidden:]) * projected[2 * hidden:3 * hidden]).astype(jnp.bfloat16)
            return (left_proj, right_proj)
        left_blocks, right_blocks = lax.map(project_rows, (split_rows(current), mask_blocks))
        left_full = join_rows(left_blocks)
        right_full = join_rows(right_blocks)
        if update == 0:

            def triangle(operands):
                return jnp.dot(operands[0], operands[1].T, preferred_element_type=jnp.float32).astype(jnp.bfloat16)
        else:

            def triangle(operands):
                return jnp.dot(operands[0].T, operands[1], preferred_element_type=jnp.float32).astype(jnp.bfloat16)
        mixed_hidden = lax.map(triangle, (left_full, right_full))

        def finish_rows(operands):
            rows_slab, mixed_rows = operands
            normed = channel_norm(rows_slab.astype(jnp.float32), input_gain[update]).astype(jnp.bfloat16)
            gate_value = jax.nn.sigmoid(jnp.einsum('dpq,de->epq', normed.astype(jnp.float32), gate_weight[update].astype(jnp.float32)))
            mixed_norm = channel_norm(mixed_rows.astype(jnp.float32), output_gain[update]).astype(jnp.bfloat16)
            update_term = jnp.einsum('dpq,de->epq', mixed_norm.astype(jnp.float32), output_weight[update].astype(jnp.float32))
            return (rows_slab.astype(jnp.float32) + gate_value * update_term).astype(jnp.bfloat16)
        current = join_rows(lax.map(finish_rows, (split_rows(current), split_rows(mixed_hidden))))
    return current
```

```python
import functools

import jax
import jax.numpy as jnp
from jax import lax
from jax.experimental import pallas as pl
from jax.experimental.pallas import tpu as pltpu
from jax.sharding import PartitionSpec as P

EPS = 1e-05
MESH = pl.DeviceIdType.MESH
F32 = jnp.float32
BF16 = jnp.bfloat16


def channel_norm(values, gain_vector):
    average = jnp.mean(values, axis=0, keepdims=True)
    centred = values - average
    spread = jnp.mean(centred * centred, axis=0, keepdims=True)
    return centred * lax.rsqrt(spread + EPS) * gain_vector[:, None, None]


def split_body(
    pair_field, residue_mask, input_gain, projection_weight, gate_weight, output_gain, output_weight
):
    rows_count = lax.axis_size("row")
    chan_count = lax.axis_size("ch")
    halves = lax.axis_size("sub")
    local_rows = pair_field.shape[1]
    local_cols = pair_field.shape[2]
    length = residue_mask.shape[0]
    hidden = output_weight.shape[1]
    per_device = hidden // (rows_count * chan_count)
    used_rows = length // halves
    half_index = lax.axis_index("sub")
    mask_float = residue_mask.astype(jnp.float32)
    row_mask = lax.dynamic_slice_in_dim(
        mask_float, (lax.axis_index("row") * halves + half_index) * local_rows, local_rows
    )
    col_mask = lax.dynamic_slice_in_dim(mask_float, lax.axis_index("ch") * local_cols, local_cols)
    pair_mask = row_mask[:, None] * col_mask[None, :]

    def arrange_rows(values):
        shaped = values.reshape(per_device, rows_count, chan_count, local_rows, local_cols)
        return shaped.transpose(0, 1, 3, 2, 4).reshape(per_device, used_rows, length)

    current = pair_field
    for update in range(2):
        normed = channel_norm(current.astype(jnp.float32), input_gain[update]).astype(jnp.bfloat16)
        projected = jnp.einsum(
            "dpq,de->epq", normed, projection_weight[update], preferred_element_type=jnp.float32
        )
        gate_value = jax.nn.sigmoid(
            jnp.einsum(
                "dpq,de->epq", normed, gate_weight[update], preferred_element_type=jnp.float32
            )
        )
        left_proj = (
            pair_mask * jax.nn.sigmoid(projected[hidden : 2 * hidden]) * projected[:hidden]
        ).astype(jnp.bfloat16)
        right_proj = (
            pair_mask * jax.nn.sigmoid(projected[3 * hidden :]) * projected[2 * hidden : 3 * hidden]
        ).astype(jnp.bfloat16)
        moved_left = lax.all_to_all(
            left_proj.reshape(hidden, 1, local_rows, local_cols),
            ("row", "ch"),
            split_axis=0,
            concat_axis=1,
            tiled=True,
        )
        moved_right = lax.all_to_all(
            right_proj.reshape(hidden, 1, local_rows, local_cols),
            ("row", "ch"),
            split_axis=0,
            concat_axis=1,
            tiled=True,
        )
        left_chan = arrange_rows(moved_left)
        right_chan = arrange_rows(moved_right)
        if update == 0:
            stacked = right_chan.reshape(per_device, rows_count, 1, local_rows, length)
            result = jnp.einsum(
                "cik,crptk->cirpt",
                left_chan,
                lax.all_gather(stacked, "sub", axis=2, tiled=True),
                preferred_element_type=jnp.float32,
            )
            mixed_hidden = result.reshape(per_device, used_rows, length).astype(jnp.bfloat16)
        else:
            left_stack = left_chan.reshape(per_device, rows_count, 1, local_rows, length)
            right_stack = right_chan.reshape(per_device, rows_count, 1, local_rows, length)
            shard_left = lax.all_gather(left_stack, "sub", axis=2, tiled=True)
            shard_right = lax.all_gather(right_stack, "sub", axis=2, tiled=True)
            span_count = shard_left.shape[2]
            accumulate_shaped = shard_left.reshape(
                per_device, rows_count, span_count, local_rows, rows_count, halves, local_rows
            )
            chosen = lax.dynamic_slice_in_dim(accumulate_shaped, half_index, 1, 5)
            chosen = chosen.reshape(per_device, rows_count, span_count, local_rows, used_rows)
            total = jnp.einsum(
                "crpti,crptj->cij", chosen, shard_right, preferred_element_type=jnp.float32
            )
            mixed_hidden = total.astype(jnp.bfloat16)
        from_shaped = mixed_hidden.reshape(
            per_device, rows_count, local_rows, chan_count, local_cols
        )
        arranged = from_shaped.transpose(0, 1, 3, 2, 4).reshape(
            per_device, rows_count * chan_count, local_rows, local_cols
        )
        returned = lax.all_to_all(arranged, ("row", "ch"), split_axis=1, concat_axis=0, tiled=True)
        mixed_rows = returned.reshape(hidden, local_rows, local_cols)
        gain_vector = output_gain[update]
        weight_rows = output_weight[update]
        mixed_norm = channel_norm(mixed_rows.astype(jnp.float32), gain_vector).astype(jnp.bfloat16)
        update_term = jnp.einsum(
            "dpq,de->epq", mixed_norm, weight_rows, preferred_element_type=jnp.float32
        )
        current = (current.astype(jnp.float32) + gate_value * update_term).astype(jnp.bfloat16)
    return current


def transposed(block):
    return block.astype(F32).T


def standardise(ref):
    channels = ref.shape[0]
    average = jnp.sum(ref[...], axis=0, keepdims=True) / channels
    spread = jnp.sum(jnp.square(ref[...] - average), axis=0, keepdims=True) / channels
    ref[...] = (ref[...] - average) * lax.rsqrt(spread + EPS)


def kernel(
    rows_count, halves,
    pair, mask, gain_in, w_proj, w_gate, gain_out, w_out, out,
    current, stage, wt, wg, wo, gcol, normed, gate, pair_mask, halfstage,
    send, recv, msend, mrecv,
    send_sem, recv_sem, msend_sem, mrecv_sem,
):
    devices = rows_count * halves
    channels, local_rows, cols = pair.shape
    own = channels // devices
    pack = own * halves
    row, sub = lax.axis_index("row"), lax.axis_index("sub")
    me = row * halves + sub

    def place(device):
        return {"row": device // halves, "sub": device % halves}

    barrier = pltpu.get_barrier_semaphore()

    def greet(step, carry):
        pl.semaphore_signal(
            barrier, inc=1, device_id=place((me + step) % devices), device_id_type=MESH
        )
        return carry

    lax.fori_loop(1, devices, greet, 0)

    current[...] = pair[...].astype(F32)
    for update in range(2):
        for kind in range(4):
            block = transposed(w_proj[update, :, kind * channels : (kind + 1) * channels])
            wt[update, :, kind * pack : (kind + 1) * pack, :] = block.reshape(
                rows_count, pack, channels
            ).astype(BF16)
        wg[update] = transposed(w_gate[update]).astype(BF16)
        wo[update] = transposed(w_out[update]).astype(BF16)
        gcol[2 * update] = jnp.broadcast_to(gain_in[update : update + 1, :], (cols, channels)).T
        gcol[2 * update + 1] = jnp.broadcast_to(
            gain_out[update : update + 1, :], (cols, channels)
        ).T
    col_mask = mask[...].astype(F32)
    lane = lax.broadcasted_iota(jnp.int32, col_mask.shape, 1)
    for r in range(local_rows):
        mine = jnp.sum(
            jnp.where(lane == me * local_rows + r, col_mask, 0.0), axis=1, keepdims=True
        )
        pair_mask[0:1, r * cols : (r + 1) * cols] = col_mask * mine

    def lr_copy(update, device, slot):
        return pltpu.make_async_remote_copy(
            src_ref=send.at[update, device],
            dst_ref=recv.at[update, slot],
            send_sem=send_sem.at[update, device],
            recv_sem=recv_sem.at[update, slot],
            device_id=place(device),
            device_id_type=MESH,
        )

    def m_copy(update, device, slot):
        return pltpu.make_async_remote_copy(
            src_ref=msend.at[update, device],
            dst_ref=mrecv.at[update, slot],
            send_sem=msend_sem.at[update, device],
            recv_sem=mrecv_sem.at[update, slot],
            device_id=place(device),
            device_id_type=MESH,
        )

    for update in range(2):
        stage[...] = current[...]
        standardise(stage)
        for r in range(local_rows):
            normed[:, r * cols : (r + 1) * cols] = (stage[:, r, :] * gcol[2 * update]).astype(BF16)

        def project(chip):
            for part in range(local_rows // 2):
                span = slice(part * 2 * cols, (part + 1) * 2 * cols)
                values = jnp.dot(wt[update, chip], normed[:, span], preferred_element_type=F32)
                masked = pair_mask[0:1, span]
                for side in range(2):
                    base = 2 * side * pack
                    scaled = (
                        masked
                        * jax.nn.sigmoid(values[base + pack : base + 2 * pack])
                        * values[base : base + pack]
                    )
                    for r in range(2):
                        halfstage[side, :, part * 2 + r, :] = scaled[:, r * cols : (r + 1) * cols]
            for half in range(halves):
                for side in range(2):
                    send[update, chip * halves + half, side] = (
                        halfstage[side, half * own : (half + 1) * own]
                        .reshape(own * local_rows, cols)
                        .astype(BF16)
                    )

        if update == 0:
            pl.semaphore_wait(barrier, devices - 1)

        def chip_step(step, carry):
            chip = (row + step) % rows_count
            project(chip)
            for half in range(halves):
                lr_copy(update, chip * halves + half, me).start()
            return carry

        lax.fori_loop(1, rows_count, chip_step, 0)
        project(row)
        for half in range(1, halves):
            lr_copy(update, row * halves + (sub + half) % halves, me).start()
        recv[update, me] = send[update, me]
        for part in range(local_rows // 2):
            span = slice(part * 2 * cols, (part + 1) * 2 * cols)
            gate[:, span] = jax.nn.sigmoid(
                jnp.dot(wg[update], normed[:, span], preferred_element_type=F32)
            )

        def lr_arrived(step, carry):
            device = (me + step) % devices
            lr_copy(update, device, device).wait_recv()
            return carry

        lax.fori_loop(1, devices, lr_arrived, 0)

        length = devices * local_rows
        contract = ((1,), (1,)) if update == 0 else ((0,), (0,))
        for couple in range(own // 2):
            span = slice(couple * 2 * local_rows, (couple + 1) * 2 * local_rows)
            sides = [
                recv[update, :, side, span, :].astype(F32).reshape(devices, 2, local_rows, cols)
                for side in range(2)
            ]
            products = []
            for c in range(2):
                left, right = (
                    values[:, c].reshape(length, cols).astype(BF16) for values in sides
                )
                product = lax.dot_general(left, right, (contract, ((), ())), preferred_element_type=F32)
                products.append(product.reshape(devices, 1, local_rows, cols))
            msend[update, :, span, :] = (
                jnp.concatenate(products, axis=1)
                .reshape(devices, 2 * local_rows, cols)
                .astype(BF16)
            )

        def m_step(step, carry):
            m_copy(update, (me + step) % devices, me).start()
            return carry

        lax.fori_loop(1, devices, m_step, 0)
        mrecv[update, me] = msend[update, me]

        def m_arrived(step, carry):
            device = (me + step) % devices
            m_copy(update, device, device).wait_recv()
            return carry

        lax.fori_loop(1, devices, m_arrived, 0)

        stage[...] = mrecv[update].astype(F32).reshape(channels, local_rows, cols)
        standardise(stage)
        for r in range(local_rows):
            normed[:, r * cols : (r + 1) * cols] = (
                stage[:, r, :] * gcol[2 * update + 1]
            ).astype(BF16)
        for part in range(local_rows // 2):
            span = slice(part * 2 * cols, (part + 1) * 2 * cols)
            term = gate[:, span] * jnp.dot(wo[update], normed[:, span], preferred_element_type=F32)
            for r in range(2):
                stage[:, part * 2 + r, :] = term[:, r * cols : (r + 1) * cols]
        fresh = (current[...] + stage[...]).astype(BF16)
        if update == 0:
            current[...] = fresh.astype(F32)
        else:
            out[...] = fresh

    def sent(step, carry):
        device = (me + step) % devices
        for update in range(2):
            lr_copy(update, device, me).wait_send()
            m_copy(update, device, me).wait_send()
        return carry

    lax.fori_loop(1, devices, sent, 0)


def fused_body(rows_count, halves, pair, mask, gain_in, w_proj, w_gate, gain_out, w_out):
    channels, local_rows, cols = pair.shape
    devices = rows_count * halves
    own = channels // devices
    slab = own * local_rows
    pack = own * halves
    wide = local_rows * cols
    vmem = pl.BlockSpec(memory_space=pltpu.VMEM)
    return pl.pallas_call(
        functools.partial(kernel, rows_count, halves),
        out_shape=jax.ShapeDtypeStruct(pair.shape, BF16),
        in_specs=[vmem] * 7,
        out_specs=vmem,
        scratch_shapes=[
            pltpu.VMEM(pair.shape, F32),
            pltpu.VMEM(pair.shape, F32),
            pltpu.VMEM((2, rows_count, 4 * pack, channels), BF16),
            pltpu.VMEM((2, channels, channels), BF16),
            pltpu.VMEM((2, channels, channels), BF16),
            pltpu.VMEM((4, channels, cols), F32),
            pltpu.VMEM((channels, wide), BF16),
            pltpu.VMEM((channels, wide), F32),
            pltpu.VMEM((8, wide), F32),
            pltpu.VMEM((2, pack, local_rows, cols), F32),
            pltpu.VMEM((2, devices, 2, slab, cols), BF16),
            pltpu.VMEM((2, devices, 2, slab, cols), BF16),
            pltpu.VMEM((2, devices, slab, cols), BF16),
            pltpu.VMEM((2, devices, slab, cols), BF16),
            pltpu.SemaphoreType.DMA((2, devices)),
            pltpu.SemaphoreType.DMA((2, devices)),
            pltpu.SemaphoreType.DMA((2, devices)),
            pltpu.SemaphoreType.DMA((2, devices)),
        ],
        compiler_params=pltpu.CompilerParams(
            collective_id=0, has_side_effects=True, vmem_limit_bytes=32 * 2**20
        ),
    )(pair, mask.reshape(1, -1), gain_in, w_proj, w_gate, gain_out, w_out)


def body(*args):
    rows_count, halves = lax.axis_size("row"), lax.axis_size("sub")
    channels, local_rows, cols = args[0].shape
    hidden = args[6].shape[1]
    devices = rows_count * halves
    fits = (
        lax.axis_size("ch") == 1
        and hidden == channels
        and devices > 1
        and local_rows == 8
        and cols == devices * local_rows
        and channels == devices * 8
        and cols % 128 == 0
    )
    if fits:
        return fused_body(rows_count, halves, *args)
    return split_body(*args)


def solution(mesh):
    placed = (P(None, ("grp", "row", "sub"), "ch"), P("grp"), P(), P(), P(), P(), P())
    return jax.shard_map(
        body,
        mesh=mesh,
        in_specs=placed,
        out_specs=P(None, ("grp", "row", "sub"), "ch"),
        check_vma=False,
    )
```

```python
import functools

import jax
import jax.numpy as jnp
from jax import lax
from jax.experimental import pallas as pl
from jax.experimental.pallas import tpu as pltpu
from jax.sharding import PartitionSpec as P

EPS = 1e-05
MESH = pl.DeviceIdType.MESH
F32 = jnp.float32
BF16 = jnp.bfloat16


def channel_norm(values, gain_vector):
    average = jnp.mean(values, axis=0, keepdims=True)
    centred = values - average
    spread = jnp.mean(centred * centred, axis=0, keepdims=True)
    return centred * lax.rsqrt(spread + EPS) * gain_vector[:, None, None]


def split_body(
    pair_field, residue_mask, input_gain, projection_weight, gate_weight, output_gain, output_weight
):
    rows_count = lax.axis_size("row")
    chan_count = lax.axis_size("ch")
    halves = lax.axis_size("sub")
    local_rows = pair_field.shape[1]
    local_cols = pair_field.shape[2]
    length = residue_mask.shape[0]
    hidden = output_weight.shape[1]
    per_device = hidden // (rows_count * chan_count)
    used_rows = length // halves
    half_index = lax.axis_index("sub")
    mask_float = residue_mask.astype(jnp.float32)
    row_mask = lax.dynamic_slice_in_dim(
        mask_float, (lax.axis_index("row") * halves + half_index) * local_rows, local_rows
    )
    col_mask = lax.dynamic_slice_in_dim(mask_float, lax.axis_index("ch") * local_cols, local_cols)
    pair_mask = row_mask[:, None] * col_mask[None, :]

    def arrange_rows(values):
        shaped = values.reshape(per_device, rows_count, chan_count, local_rows, local_cols)
        return shaped.transpose(0, 1, 3, 2, 4).reshape(per_device, used_rows, length)

    current = pair_field
    for update in range(2):
        normed = channel_norm(current.astype(jnp.float32), input_gain[update]).astype(jnp.bfloat16)
        projected = jnp.einsum(
            "dpq,de->epq", normed, projection_weight[update], preferred_element_type=jnp.float32
        )
        gate_value = jax.nn.sigmoid(
            jnp.einsum(
                "dpq,de->epq", normed, gate_weight[update], preferred_element_type=jnp.float32
            )
        )
        left_proj = (
            pair_mask * jax.nn.sigmoid(projected[hidden : 2 * hidden]) * projected[:hidden]
        ).astype(jnp.bfloat16)
        right_proj = (
            pair_mask * jax.nn.sigmoid(projected[3 * hidden :]) * projected[2 * hidden : 3 * hidden]
        ).astype(jnp.bfloat16)
        moved_left = lax.all_to_all(
            left_proj.reshape(hidden, 1, local_rows, local_cols),
            ("row", "ch"),
            split_axis=0,
            concat_axis=1,
            tiled=True,
        )
        moved_right = lax.all_to_all(
            right_proj.reshape(hidden, 1, local_rows, local_cols),
            ("row", "ch"),
            split_axis=0,
            concat_axis=1,
            tiled=True,
        )
        left_chan = arrange_rows(moved_left)
        right_chan = arrange_rows(moved_right)
        if update == 0:
            stacked = right_chan.reshape(per_device, rows_count, 1, local_rows, length)
            result = jnp.einsum(
                "cik,crptk->cirpt",
                left_chan,
                lax.all_gather(stacked, "sub", axis=2, tiled=True),
                preferred_element_type=jnp.float32,
            )
            mixed_hidden = result.reshape(per_device, used_rows, length).astype(jnp.bfloat16)
        else:
            left_stack = left_chan.reshape(per_device, rows_count, 1, local_rows, length)
            right_stack = right_chan.reshape(per_device, rows_count, 1, local_rows, length)
            shard_left = lax.all_gather(left_stack, "sub", axis=2, tiled=True)
            shard_right = lax.all_gather(right_stack, "sub", axis=2, tiled=True)
            span_count = shard_left.shape[2]
            accumulate_shaped = shard_left.reshape(
                per_device, rows_count, span_count, local_rows, rows_count, halves, local_rows
            )
            chosen = lax.dynamic_slice_in_dim(accumulate_shaped, half_index, 1, 5)
            chosen = chosen.reshape(per_device, rows_count, span_count, local_rows, used_rows)
            total = jnp.einsum(
                "crpti,crptj->cij", chosen, shard_right, preferred_element_type=jnp.float32
            )
            mixed_hidden = total.astype(jnp.bfloat16)
        from_shaped = mixed_hidden.reshape(
            per_device, rows_count, local_rows, chan_count, local_cols
        )
        arranged = from_shaped.transpose(0, 1, 3, 2, 4).reshape(
            per_device, rows_count * chan_count, local_rows, local_cols
        )
        returned = lax.all_to_all(arranged, ("row", "ch"), split_axis=1, concat_axis=0, tiled=True)
        mixed_rows = returned.reshape(hidden, local_rows, local_cols)
        gain_vector = output_gain[update]
        weight_rows = output_weight[update]
        mixed_norm = channel_norm(mixed_rows.astype(jnp.float32), gain_vector).astype(jnp.bfloat16)
        update_term = jnp.einsum(
            "dpq,de->epq", mixed_norm, weight_rows, preferred_element_type=jnp.float32
        )
        current = (current.astype(jnp.float32) + gate_value * update_term).astype(jnp.bfloat16)
    return current


def transposed(block):
    return block.astype(F32).T


def moments(ref):
    channels, chunk = ref.shape[0], 16
    total = jnp.zeros(ref.shape[1:], F32)
    for start in range(0, channels, chunk):
        total = total + jnp.sum(ref[start : start + chunk], axis=0)
    average = total / channels
    total = jnp.zeros(ref.shape[1:], F32)
    for start in range(0, channels, chunk):
        total = total + jnp.sum(jnp.square(ref[start : start + chunk] - average), axis=0)
    return average, lax.rsqrt(total / channels + EPS)


def kernel(
    rows_count, halves,
    pair_hbm, mask_hbm, gain_in_hbm, w_proj_hbm, w_gate_hbm, gain_out_hbm, w_out_hbm, out,
    pair, mask, gain_in, w_proj, w_gate, gain_out, w_out,
    current, stage, wt, wg, wo, gcol, normed, gate, pair_mask, slab_stage,
    send, recv, msend, mrecv,
    in_sem, send_sem, recv_sem, msend_sem, mrecv_sem,
):
    devices = rows_count * halves
    channels, local_rows, cols = pair.shape
    plane = 4
    planes = devices // plane
    own = channels // devices // 2
    pack = own * plane
    half_channels = channels // 2
    row, sub = lax.axis_index("row"), lax.axis_index("sub")
    me = row * halves + sub
    my_plane = me // plane
    my_seat = me % plane

    fetches = [
        pltpu.make_async_copy(src, dst, in_sem.at[index])
        for index, (src, dst) in enumerate(
            (
                (pair_hbm, pair),
                (w_proj_hbm, w_proj),
                (gain_in_hbm, gain_in),
                (mask_hbm, mask),
                (w_gate_hbm, w_gate),
                (gain_out_hbm, gain_out),
                (w_out_hbm, w_out),
            )
        )
    ]
    for fetch in fetches:
        fetch.start()

    def place(device):
        return {"row": device // halves, "sub": device % halves}

    barrier = pltpu.get_barrier_semaphore()

    def greet(step, carry):
        pl.semaphore_signal(
            barrier, inc=1, device_id=place((me + step) % devices), device_id_type=MESH
        )
        return carry

    lax.fori_loop(1, devices, greet, 0)

    def prepare_projection(update):
        for kind in range(4):
            block = transposed(w_proj[update, :, kind * channels : (kind + 1) * channels])
            wt[update, :, kind * pack : (kind + 1) * pack, :] = block.reshape(
                2 * planes, pack, channels
            ).astype(BF16)
        gcol[2 * update] = jnp.broadcast_to(gain_in[update : update + 1, :], (cols, channels)).T

    def prepare_finish(update):
        wo[update] = transposed(w_out[update]).astype(BF16)
        gcol[2 * update + 1] = jnp.broadcast_to(
            gain_out[update : update + 1, :], (cols, channels)
        ).T

    for fetch in fetches[:4]:
        fetch.wait()
    current[...] = pair[...].astype(F32)
    prepare_projection(0)
    col_mask = mask[...].astype(F32)
    lane = lax.broadcasted_iota(jnp.int32, col_mask.shape, 1)
    for r in range(local_rows):
        mine = jnp.sum(
            jnp.where(lane == me * local_rows + r, col_mask, 0.0), axis=1, keepdims=True
        )
        pair_mask[0:1, r * cols : (r + 1) * cols] = col_mask * mine

    def lr_copy(update, half, device, slot):
        return pltpu.make_async_remote_copy(
            src_ref=send.at[update, half, device],
            dst_ref=recv.at[update, half, slot],
            send_sem=send_sem.at[update, half, device],
            recv_sem=recv_sem.at[update, half, slot],
            device_id=place(device),
            device_id_type=MESH,
        )

    def m_copy(update, half, device, slot):
        return pltpu.make_async_remote_copy(
            src_ref=msend.at[update, half, device],
            dst_ref=mrecv.at[update, half, slot],
            send_sem=msend_sem.at[update, half, device],
            recv_sem=mrecv_sem.at[update, half, slot],
            device_id=place(device),
            device_id_type=MESH,
        )

    def normalise(ref, gains):
        average, scale = moments(ref)
        for r in range(local_rows):
            normed[:, r * cols : (r + 1) * cols] = (
                (ref[:, r, :] - average[r : r + 1]) * scale[r : r + 1] * gcol[gains]
            ).astype(BF16)

    for update in range(2):
        normalise(current, 2 * update)

        def project(half, group):
            for part in range(local_rows // 2):
                span = slice(part * 2 * cols, (part + 1) * 2 * cols)
                values = jnp.dot(
                    wt[update, half * planes + group], normed[:, span], preferred_element_type=F32
                )
                masked = pair_mask[0:1, span]
                for side in range(2):
                    base = 2 * side * pack
                    scaled = (
                        masked
                        * jax.nn.sigmoid(values[base + pack : base + 2 * pack])
                        * values[base : base + pack]
                    )
                    for r in range(2):
                        slab_stage[side, :, part * 2 + r, :] = scaled[:, r * cols : (r + 1) * cols]
            for seat in range(plane):
                for side in range(2):
                    send[update, half, group * plane + seat, side] = (
                        slab_stage[side, seat * own : (seat + 1) * own]
                        .reshape(own * local_rows, cols)
                        .astype(BF16)
                    )

        if update == 0:
            pl.semaphore_wait(barrier, devices - 1)

        for half in range(2):

            def plane_step(step, carry):
                group = (my_plane + step) % planes
                project(half, group)
                for seat in range(plane):
                    lr_copy(update, half, group * plane + (my_seat + seat) % plane, me).start()
                return carry

            lax.fori_loop(1, planes, plane_step, 0)
            project(half, my_plane)
            for seat in range(1, plane):
                lr_copy(update, half, my_plane * plane + (my_seat + seat) % plane, me).start()
            recv[update, half, me] = send[update, half, me]

        if update == 0:
            for fetch in fetches[4:]:
                fetch.wait()
            for later in range(2):
                wg[later] = transposed(w_gate[later]).astype(BF16)
        for part in range(local_rows // 2):
            span = slice(part * 2 * cols, (part + 1) * 2 * cols)
            gate[:, span] = jax.nn.sigmoid(
                jnp.dot(wg[update], normed[:, span], preferred_element_type=F32)
            )
        if update == 0:
            prepare_finish(0)
            prepare_projection(1)
            prepare_finish(1)

        length = devices * local_rows
        contract = ((1,), (1,)) if update == 0 else ((0,), (0,))
        for half in range(2):

            def lr_arrived(step, carry):
                device = (me + step) % devices
                lr_copy(update, half, device, device).wait_recv()
                return carry

            lax.fori_loop(1, devices, lr_arrived, 0)
            for couple in range(own // 2):
                span = slice(couple * 2 * local_rows, (couple + 1) * 2 * local_rows)
                sides = [
                    recv[update, half, :, side, span, :]
                    .astype(F32)
                    .reshape(devices, 2, local_rows, cols)
                    for side in range(2)
                ]
                products = []
                for c in range(2):
                    left, right = (
                        values[:, c].reshape(length, cols).astype(BF16) for values in sides
                    )
                    product = lax.dot_general(
                        left, right, (contract, ((), ())), preferred_element_type=F32
                    )
                    products.append(product.reshape(devices, 1, local_rows, cols))
                msend[update, half, :, span, :] = (
                    jnp.concatenate(products, axis=1)
                    .reshape(devices, 2 * local_rows, cols)
                    .astype(BF16)
                )

            def m_step(step, carry):
                m_copy(update, half, (me + step) % devices, me).start()
                return carry

            lax.fori_loop(1, devices, m_step, 0)
            mrecv[update, half, me] = msend[update, half, me]

        for half in range(2):

            def m_arrived(step, carry):
                device = (me + step) % devices
                m_copy(update, half, device, device).wait_recv()
                return carry

            lax.fori_loop(1, devices, m_arrived, 0)
            stage[half * half_channels : (half + 1) * half_channels] = (
                mrecv[update, half].astype(F32).reshape(half_channels, local_rows, cols)
            )

        normalise(stage, 2 * update + 1)
        for part in range(local_rows // 2):
            span = slice(part * 2 * cols, (part + 1) * 2 * cols)
            term = gate[:, span] * jnp.dot(wo[update], normed[:, span], preferred_element_type=F32)
            for r in range(2):
                stage[:, part * 2 + r, :] = term[:, r * cols : (r + 1) * cols]
        fresh = (current[...] + stage[...]).astype(BF16)
        if update == 0:
            current[...] = fresh.astype(F32)
        else:
            out[...] = fresh

    def sent(step, carry):
        device = (me + step) % devices
        for update in range(2):
            for half in range(2):
                lr_copy(update, half, device, me).wait_send()
                m_copy(update, half, device, me).wait_send()
        return carry

    lax.fori_loop(1, devices, sent, 0)


def fused_body(rows_count, halves, pair, mask, gain_in, w_proj, w_gate, gain_out, w_out):
    channels, local_rows, cols = pair.shape
    devices = rows_count * halves
    own = channels // devices // 2
    slab = own * local_rows
    pack = own * 4
    wide = local_rows * cols
    operands = (pair, mask.reshape(1, -1), gain_in, w_proj, w_gate, gain_out, w_out)
    vmem = pl.BlockSpec(memory_space=pltpu.VMEM)
    hbm = pl.BlockSpec(memory_space=pltpu.HBM)
    return pl.pallas_call(
        functools.partial(kernel, rows_count, halves),
        out_shape=jax.ShapeDtypeStruct(pair.shape, BF16),
        in_specs=[hbm] * 7,
        out_specs=vmem,
        scratch_shapes=[pltpu.VMEM(each.shape, each.dtype) for each in operands]
        + [
            pltpu.VMEM(pair.shape, F32),
            pltpu.VMEM(pair.shape, F32),
            pltpu.VMEM((2, devices // 2, 4 * pack, channels), BF16),
            pltpu.VMEM((2, channels, channels), BF16),
            pltpu.VMEM((2, channels, channels), BF16),
            pltpu.VMEM((4, channels, cols), F32),
            pltpu.VMEM((channels, wide), BF16),
            pltpu.VMEM((channels, wide), F32),
            pltpu.VMEM((8, wide), F32),
            pltpu.VMEM((2, pack, local_rows, cols), F32),
            pltpu.VMEM((2, 2, devices, 2, slab, cols), BF16),
            pltpu.VMEM((2, 2, devices, 2, slab, cols), BF16),
            pltpu.VMEM((2, 2, devices, slab, cols), BF16),
            pltpu.VMEM((2, 2, devices, slab, cols), BF16),
            pltpu.SemaphoreType.DMA((7,)),
            pltpu.SemaphoreType.DMA((2, 2, devices)),
            pltpu.SemaphoreType.DMA((2, 2, devices)),
            pltpu.SemaphoreType.DMA((2, 2, devices)),
            pltpu.SemaphoreType.DMA((2, 2, devices)),
        ],
        compiler_params=pltpu.CompilerParams(
            collective_id=0, has_side_effects=True, vmem_limit_bytes=60 * 2**20
        ),
    )(*operands)


def body(*args):
    rows_count, halves = lax.axis_size("row"), lax.axis_size("sub")
    channels, local_rows, cols = args[0].shape
    hidden = args[6].shape[1]
    devices = rows_count * halves
    fits = (
        lax.axis_size("ch") == 1
        and hidden == channels
        and devices % 4 == 0
        and local_rows == 8
        and cols == devices * local_rows
        and channels == devices * 8
        and cols % 128 == 0
    )
    if fits:
        return fused_body(rows_count, halves, *args)
    return split_body(*args)


def solution(mesh):
    placed = (P(None, ("grp", "row", "sub"), "ch"), P("grp"), P(), P(), P(), P(), P())
    return jax.shard_map(
        body,
        mesh=mesh,
        in_specs=placed,
        out_specs=P(None, ("grp", "row", "sub"), "ch"),
        check_vma=False,
    )
```

```python
import functools

import jax
import jax.numpy as jnp
from jax import lax
from jax.experimental import pallas as pl
from jax.experimental.pallas import tpu as pltpu
from jax.sharding import PartitionSpec as P

EPS = 1e-05
MESH = pl.DeviceIdType.MESH
F32 = jnp.float32
BF16 = jnp.bfloat16


def channel_norm(values, gain_vector):
    average = jnp.mean(values, axis=0, keepdims=True)
    centred = values - average
    spread = jnp.mean(centred * centred, axis=0, keepdims=True)
    return centred * lax.rsqrt(spread + EPS) * gain_vector[:, None, None]


def split_body(
    pair_field, residue_mask, input_gain, projection_weight, gate_weight, output_gain, output_weight
):
    rows_count = lax.axis_size("row")
    chan_count = lax.axis_size("ch")
    halves = lax.axis_size("sub")
    local_rows = pair_field.shape[1]
    local_cols = pair_field.shape[2]
    length = residue_mask.shape[0]
    hidden = output_weight.shape[1]
    per_device = hidden // (rows_count * chan_count)
    used_rows = length // halves
    half_index = lax.axis_index("sub")
    mask_float = residue_mask.astype(jnp.float32)
    row_mask = lax.dynamic_slice_in_dim(
        mask_float, (lax.axis_index("row") * halves + half_index) * local_rows, local_rows
    )
    col_mask = lax.dynamic_slice_in_dim(mask_float, lax.axis_index("ch") * local_cols, local_cols)
    pair_mask = row_mask[:, None] * col_mask[None, :]

    def arrange_rows(values):
        shaped = values.reshape(per_device, rows_count, chan_count, local_rows, local_cols)
        return shaped.transpose(0, 1, 3, 2, 4).reshape(per_device, used_rows, length)

    current = pair_field
    for update in range(2):
        normed = channel_norm(current.astype(jnp.float32), input_gain[update]).astype(jnp.bfloat16)
        projected = jnp.einsum(
            "dpq,de->epq", normed, projection_weight[update], preferred_element_type=jnp.float32
        )
        gate_value = jax.nn.sigmoid(
            jnp.einsum(
                "dpq,de->epq", normed, gate_weight[update], preferred_element_type=jnp.float32
            )
        )
        left_proj = (
            pair_mask * jax.nn.sigmoid(projected[hidden : 2 * hidden]) * projected[:hidden]
        ).astype(jnp.bfloat16)
        right_proj = (
            pair_mask * jax.nn.sigmoid(projected[3 * hidden :]) * projected[2 * hidden : 3 * hidden]
        ).astype(jnp.bfloat16)
        moved_left = lax.all_to_all(
            left_proj.reshape(hidden, 1, local_rows, local_cols),
            ("row", "ch"),
            split_axis=0,
            concat_axis=1,
            tiled=True,
        )
        moved_right = lax.all_to_all(
            right_proj.reshape(hidden, 1, local_rows, local_cols),
            ("row", "ch"),
            split_axis=0,
            concat_axis=1,
            tiled=True,
        )
        left_chan = arrange_rows(moved_left)
        right_chan = arrange_rows(moved_right)
        if update == 0:
            stacked = right_chan.reshape(per_device, rows_count, 1, local_rows, length)
            result = jnp.einsum(
                "cik,crptk->cirpt",
                left_chan,
                lax.all_gather(stacked, "sub", axis=2, tiled=True),
                preferred_element_type=jnp.float32,
            )
            mixed_hidden = result.reshape(per_device, used_rows, length).astype(jnp.bfloat16)
        else:
            left_stack = left_chan.reshape(per_device, rows_count, 1, local_rows, length)
            right_stack = right_chan.reshape(per_device, rows_count, 1, local_rows, length)
            shard_left = lax.all_gather(left_stack, "sub", axis=2, tiled=True)
            shard_right = lax.all_gather(right_stack, "sub", axis=2, tiled=True)
            span_count = shard_left.shape[2]
            accumulate_shaped = shard_left.reshape(
                per_device, rows_count, span_count, local_rows, rows_count, halves, local_rows
            )
            chosen = lax.dynamic_slice_in_dim(accumulate_shaped, half_index, 1, 5)
            chosen = chosen.reshape(per_device, rows_count, span_count, local_rows, used_rows)
            total = jnp.einsum(
                "crpti,crptj->cij", chosen, shard_right, preferred_element_type=jnp.float32
            )
            mixed_hidden = total.astype(jnp.bfloat16)
        from_shaped = mixed_hidden.reshape(
            per_device, rows_count, local_rows, chan_count, local_cols
        )
        arranged = from_shaped.transpose(0, 1, 3, 2, 4).reshape(
            per_device, rows_count * chan_count, local_rows, local_cols
        )
        returned = lax.all_to_all(arranged, ("row", "ch"), split_axis=1, concat_axis=0, tiled=True)
        mixed_rows = returned.reshape(hidden, local_rows, local_cols)
        gain_vector = output_gain[update]
        weight_rows = output_weight[update]
        mixed_norm = channel_norm(mixed_rows.astype(jnp.float32), gain_vector).astype(jnp.bfloat16)
        update_term = jnp.einsum(
            "dpq,de->epq", mixed_norm, weight_rows, preferred_element_type=jnp.float32
        )
        current = (current.astype(jnp.float32) + gate_value * update_term).astype(jnp.bfloat16)
    return current


def transposed(block):
    return block.astype(F32).T


def moments(ref):
    channels, chunk = ref.shape[0], 16
    total = jnp.zeros(ref.shape[1:], F32)
    for start in range(0, channels, chunk):
        total = total + jnp.sum(ref[start : start + chunk], axis=0)
    average = total / channels
    total = jnp.zeros(ref.shape[1:], F32)
    for start in range(0, channels, chunk):
        total = total + jnp.sum(jnp.square(ref[start : start + chunk] - average), axis=0)
    return average, lax.rsqrt(total / channels + EPS)


def kernel(
    rows_count, halves,
    pair_hbm, mask_hbm, gain_in_hbm, w_proj_hbm, w_gate_hbm, gain_out_hbm, w_out_hbm, out,
    pair, mask, gain_in, w_proj, w_gate, gain_out, w_out,
    current, stage, wt, wg, wo, gcol, normed, gate, pair_mask, slab_stage,
    lsend, rsend, lrecv, rrecv, msend, mrecv,
    in_sem, lsend_sem, lrecv_sem, rsend_sem, rrecv_sem, msend_sem, mrecv_sem,
):
    devices = rows_count * halves
    channels, local_rows, cols = pair.shape
    camp = devices // 2
    plane = 4
    planes = camp // plane
    own = channels // camp // 2
    pack = own * plane
    half_channels = channels // 2
    row, sub = lax.axis_index("row"), lax.axis_index("sub")
    me = row * halves + sub
    my_base = (me // camp) * camp
    far_base = camp - my_base
    my_rank = me % camp
    my_plane = my_rank // plane
    my_seat = my_rank % plane

    fetches = [
        pltpu.make_async_copy(src, dst, in_sem.at[index])
        for index, (src, dst) in enumerate(
            (
                (pair_hbm, pair),
                (w_proj_hbm, w_proj),
                (gain_in_hbm, gain_in),
                (mask_hbm, mask),
                (w_gate_hbm, w_gate),
                (gain_out_hbm, gain_out),
                (w_out_hbm, w_out),
            )
        )
    ]
    for fetch in fetches:
        fetch.start()

    def place(device):
        return {"row": device // halves, "sub": device % halves}

    barrier = pltpu.get_barrier_semaphore()

    def greet(step, carry):
        pl.semaphore_signal(
            barrier, inc=1, device_id=place((me + step) % devices), device_id_type=MESH
        )
        return carry

    lax.fori_loop(1, devices, greet, 0)

    def prepare_projection(update):
        for kind in range(4):
            block = transposed(w_proj[update, :, kind * channels : (kind + 1) * channels])
            wt[update, :, kind * pack : (kind + 1) * pack, :] = block.reshape(
                2 * planes, pack, channels
            ).astype(BF16)
        gcol[2 * update] = jnp.broadcast_to(gain_in[update : update + 1, :], (cols, channels)).T

    def prepare_finish(update):
        wo[update] = transposed(w_out[update]).astype(BF16)
        gcol[2 * update + 1] = jnp.broadcast_to(
            gain_out[update : update + 1, :], (cols, channels)
        ).T

    for fetch in fetches[:4]:
        fetch.wait()
    current[...] = pair[...].astype(F32)
    prepare_projection(0)
    col_mask = mask[...].astype(F32)
    lane = lax.broadcasted_iota(jnp.int32, col_mask.shape, 1)
    for r in range(local_rows):
        mine = jnp.sum(
            jnp.where(lane == me * local_rows + r, col_mask, 0.0), axis=1, keepdims=True
        )
        pair_mask[0:1, r * cols : (r + 1) * cols] = col_mask * mine

    def l_copy(update, half, device, slot):
        return pltpu.make_async_remote_copy(
            src_ref=lsend.at[update, half, device % camp],
            dst_ref=lrecv.at[update, half, slot],
            send_sem=lsend_sem.at[update, half, device % camp],
            recv_sem=lrecv_sem.at[update, half, slot],
            device_id=place(device),
            device_id_type=MESH,
        )

    def r_copy(update, half, device, slot):
        return pltpu.make_async_remote_copy(
            src_ref=rsend.at[update, half, device % camp],
            dst_ref=rrecv.at[update, half, slot],
            send_sem=rsend_sem.at[update, half, device],
            recv_sem=rrecv_sem.at[update, half, slot],
            device_id=place(device),
            device_id_type=MESH,
        )

    def m_copy(update, half, device, slot):
        return pltpu.make_async_remote_copy(
            src_ref=msend.at[update, half, device],
            dst_ref=mrecv.at[update, half, slot],
            send_sem=msend_sem.at[update, half, device],
            recv_sem=mrecv_sem.at[update, half, slot],
            device_id=place(device),
            device_id_type=MESH,
        )

    def normalise(ref, gains):
        average, scale = moments(ref)
        for r in range(local_rows):
            normed[:, r * cols : (r + 1) * cols] = (
                (ref[:, r, :] - average[r : r + 1]) * scale[r : r + 1] * gcol[gains]
            ).astype(BF16)

    for update in range(2):
        normalise(current, 2 * update)

        def project(half, group):
            for part in range(local_rows // 2):
                span = slice(part * 2 * cols, (part + 1) * 2 * cols)
                values = jnp.dot(
                    wt[update, half * planes + group], normed[:, span], preferred_element_type=F32
                )
                masked = pair_mask[0:1, span]
                for side in range(2):
                    base = 2 * side * pack
                    scaled = (
                        masked
                        * jax.nn.sigmoid(values[base + pack : base + 2 * pack])
                        * values[base : base + pack]
                    )
                    for r in range(2):
                        slab_stage[side, :, part * 2 + r, :] = scaled[:, r * cols : (r + 1) * cols]
            for seat in range(plane):
                for side, target in enumerate((lsend, rsend)):
                    target[update, half, group * plane + seat] = (
                        slab_stage[side, seat * own : (seat + 1) * own]
                        .reshape(own * local_rows, cols)
                        .astype(BF16)
                    )

        if update == 0:
            pl.semaphore_wait(barrier, devices - 1)

        r_slot = me if update == 0 else my_rank
        for half in range(2):
            for step in range(1, planes + 1):
                group = (my_plane + step) % planes
                project(half, group)
                for seat in range(plane):
                    rank = group * plane + (my_seat + seat) % plane
                    if update == 0:
                        r_copy(update, half, far_base + rank, r_slot).start()
                    if step < planes or seat > 0:
                        l_copy(update, half, my_base + rank, my_rank).start()
                        r_copy(update, half, my_base + rank, r_slot).start()
            lrecv[update, half, my_rank] = lsend[update, half, my_rank]
            rrecv[update, half, r_slot] = rsend[update, half, my_rank]

        if update == 0:
            for fetch in fetches[4:]:
                fetch.wait()
            for later in range(2):
                wg[later] = transposed(w_gate[later]).astype(BF16)
        for part in range(local_rows // 2):
            span = slice(part * 2 * cols, (part + 1) * 2 * cols)
            gate[:, span] = jax.nn.sigmoid(
                jnp.dot(wg[update], normed[:, span], preferred_element_type=F32)
            )
        if update == 0:
            prepare_finish(0)
            prepare_projection(1)
            prepare_finish(1)

        contract = ((1,), (1,)) if update == 0 else ((0,), (0,))
        sources = devices if update == 0 else camp
        targets = camp if update == 0 else devices
        for half in range(2):

            def near_arrived(step, carry):
                rank = (my_rank + step) % camp
                l_copy(update, half, my_base + rank, rank).wait_recv()
                slot = my_base + rank if update == 0 else rank
                r_copy(update, half, my_base + rank, slot).wait_recv()
                return carry

            lax.fori_loop(1, camp, near_arrived, 0)
            if update == 0:

                def far_arrived(step, carry):
                    device = far_base + (my_rank + step) % camp
                    r_copy(update, half, device, device).wait_recv()
                    return carry

                lax.fori_loop(0, camp, far_arrived, 0)
            for couple in range(own // 2):
                span = slice(couple * 2 * local_rows, (couple + 1) * 2 * local_rows)
                lefts = lrecv[update, half, :, span, :].astype(F32)
                lefts = lefts.reshape(camp, 2, local_rows, cols)
                rights = rrecv[update, half, :sources, span, :].astype(F32)
                rights = rights.reshape(sources, 2, local_rows, cols)
                products = []
                for c in range(2):
                    product = lax.dot_general(
                        lefts[:, c].reshape(camp * local_rows, cols).astype(BF16),
                        rights[:, c].reshape(sources * local_rows, cols).astype(BF16),
                        (contract, ((), ())),
                        preferred_element_type=F32,
                    )
                    products.append(product.reshape(targets, 1, local_rows, cols))
                block = (
                    jnp.concatenate(products, axis=1)
                    .reshape(targets, 2 * local_rows, cols)
                    .astype(BF16)
                )
                if update == 0:
                    msend[update, half, pl.ds(my_base, camp), span, :] = block
                else:
                    msend[update, half, :, span, :] = block

            if update == 1:

                def m_far(step, carry):
                    rank = (my_rank + step) % camp
                    m_copy(update, half, far_base + rank, camp + my_rank).start()
                    return carry

                lax.fori_loop(0, camp, m_far, 0)

            def m_near(step, carry):
                rank = (my_rank + step) % camp
                m_copy(update, half, my_base + rank, my_rank).start()
                return carry

            lax.fori_loop(1, camp, m_near, 0)
            mrecv[update, half, my_rank] = msend[update, half, me]

        for half in range(2):

            def m_arrived(step, carry):
                rank = (my_rank + step) % camp
                m_copy(update, half, my_base + rank, rank).wait_recv()
                return carry

            lax.fori_loop(1, camp, m_arrived, 0)
            mixed = mrecv[update, half, :camp].astype(F32)
            if update == 1:

                def m_far_arrived(step, carry):
                    rank = (my_rank + step) % camp
                    m_copy(update, half, far_base + rank, camp + rank).wait_recv()
                    return carry

                lax.fori_loop(0, camp, m_far_arrived, 0)
                mixed = mixed + mrecv[update, half, camp:].astype(F32)
            stage[half * half_channels : (half + 1) * half_channels] = mixed.reshape(
                half_channels, local_rows, cols
            )

        normalise(stage, 2 * update + 1)
        for part in range(local_rows // 2):
            span = slice(part * 2 * cols, (part + 1) * 2 * cols)
            term = gate[:, span] * jnp.dot(wo[update], normed[:, span], preferred_element_type=F32)
            for r in range(2):
                stage[:, part * 2 + r, :] = term[:, r * cols : (r + 1) * cols]
        fresh = (current[...] + stage[...]).astype(BF16)
        if update == 0:
            current[...] = fresh.astype(F32)
        else:
            out[...] = fresh

    for update in range(2):
        for half in range(2):

            def near_sent(step, carry):
                device = my_base + (my_rank + step) % camp
                l_copy(update, half, device, my_rank).wait_send()
                r_copy(update, half, device, my_rank).wait_send()
                m_copy(update, half, device, my_rank).wait_send()
                return carry

            lax.fori_loop(1, camp, near_sent, 0)

            def far_sent(step, carry):
                device = far_base + (my_rank + step) % camp
                if update == 0:
                    r_copy(update, half, device, me).wait_send()
                else:
                    m_copy(update, half, device, camp + my_rank).wait_send()
                return carry

            lax.fori_loop(0, camp, far_sent, 0)


def fused_body(rows_count, halves, pair, mask, gain_in, w_proj, w_gate, gain_out, w_out):
    channels, local_rows, cols = pair.shape
    devices = rows_count * halves
    camp = devices // 2
    own = channels // camp // 2
    slab = own * local_rows
    pack = own * 4
    wide = local_rows * cols
    operands = (pair, mask.reshape(1, -1), gain_in, w_proj, w_gate, gain_out, w_out)
    vmem = pl.BlockSpec(memory_space=pltpu.VMEM)
    hbm = pl.BlockSpec(memory_space=pltpu.HBM)
    return pl.pallas_call(
        functools.partial(kernel, rows_count, halves),
        out_shape=jax.ShapeDtypeStruct(pair.shape, BF16),
        in_specs=[hbm] * 7,
        out_specs=vmem,
        scratch_shapes=[pltpu.VMEM(each.shape, each.dtype) for each in operands]
        + [
            pltpu.VMEM(pair.shape, F32),
            pltpu.VMEM(pair.shape, F32),
            pltpu.VMEM((2, camp // 2, 4 * pack, channels), BF16),
            pltpu.VMEM((2, channels, channels), BF16),
            pltpu.VMEM((2, channels, channels), BF16),
            pltpu.VMEM((4, channels, cols), F32),
            pltpu.VMEM((channels, wide), BF16),
            pltpu.VMEM((channels, wide), F32),
            pltpu.VMEM((8, wide), F32),
            pltpu.VMEM((2, pack, local_rows, cols), F32),
            pltpu.VMEM((2, 2, camp, slab, cols), BF16),
            pltpu.VMEM((2, 2, camp, slab, cols), BF16),
            pltpu.VMEM((2, 2, camp, slab, cols), BF16),
            pltpu.VMEM((2, 2, devices, slab, cols), BF16),
            pltpu.VMEM((2, 2, devices, slab, cols), BF16),
            pltpu.VMEM((2, 2, devices, slab, cols), BF16),
            pltpu.SemaphoreType.DMA((7,)),
            pltpu.SemaphoreType.DMA((2, 2, camp)),
            pltpu.SemaphoreType.DMA((2, 2, camp)),
            pltpu.SemaphoreType.DMA((2, 2, devices)),
            pltpu.SemaphoreType.DMA((2, 2, devices)),
            pltpu.SemaphoreType.DMA((2, 2, devices)),
            pltpu.SemaphoreType.DMA((2, 2, devices)),
        ],
        compiler_params=pltpu.CompilerParams(
            collective_id=0, has_side_effects=True, vmem_limit_bytes=60 * 2**20
        ),
    )(*operands)


def body(*args):
    rows_count, halves = lax.axis_size("row"), lax.axis_size("sub")
    channels, local_rows, cols = args[0].shape
    hidden = args[6].shape[1]
    devices = rows_count * halves
    fits = (
        lax.axis_size("ch") == 1
        and hidden == channels
        and devices % 8 == 0
        and local_rows == 8
        and cols == devices * local_rows
        and channels == devices * 8
        and cols % 128 == 0
    )
    if fits:
        return fused_body(rows_count, halves, *args)
    return split_body(*args)


def solution(mesh):
    placed = (P(None, ("grp", "row", "sub"), "ch"), P("grp"), P(), P(), P(), P(), P())
    return jax.shard_map(
        body,
        mesh=mesh,
        in_specs=placed,
        out_specs=P(None, ("grp", "row", "sub"), "ch"),
        check_vma=False,
    )
```

```python
import functools

import jax
import jax.numpy as jnp
from jax import lax
from jax.experimental import pallas as pl
from jax.experimental.pallas import tpu as pltpu
from jax.sharding import PartitionSpec as P

EPS = 1e-05
MESH = pl.DeviceIdType.MESH
F32 = jnp.float32
BF16 = jnp.bfloat16


def channel_norm(values, gain_vector):
    average = jnp.mean(values, axis=0, keepdims=True)
    centred = values - average
    spread = jnp.mean(centred * centred, axis=0, keepdims=True)
    return centred * lax.rsqrt(spread + EPS) * gain_vector[:, None, None]


def split_body(
    pair_field, residue_mask, input_gain, projection_weight, gate_weight, output_gain, output_weight
):
    rows_count = lax.axis_size("row")
    chan_count = lax.axis_size("ch")
    halves = lax.axis_size("sub")
    local_rows = pair_field.shape[1]
    local_cols = pair_field.shape[2]
    length = residue_mask.shape[0]
    hidden = output_weight.shape[1]
    per_device = hidden // (rows_count * chan_count)
    used_rows = length // halves
    half_index = lax.axis_index("sub")
    mask_float = residue_mask.astype(jnp.float32)
    row_mask = lax.dynamic_slice_in_dim(
        mask_float, (lax.axis_index("row") * halves + half_index) * local_rows, local_rows
    )
    col_mask = lax.dynamic_slice_in_dim(mask_float, lax.axis_index("ch") * local_cols, local_cols)
    pair_mask = row_mask[:, None] * col_mask[None, :]

    def arrange_rows(values):
        shaped = values.reshape(per_device, rows_count, chan_count, local_rows, local_cols)
        return shaped.transpose(0, 1, 3, 2, 4).reshape(per_device, used_rows, length)

    current = pair_field
    for update in range(2):
        normed = channel_norm(current.astype(jnp.float32), input_gain[update]).astype(jnp.bfloat16)
        projected = jnp.einsum(
            "dpq,de->epq", normed, projection_weight[update], preferred_element_type=jnp.float32
        )
        gate_value = jax.nn.sigmoid(
            jnp.einsum(
                "dpq,de->epq", normed, gate_weight[update], preferred_element_type=jnp.float32
            )
        )
        left_proj = (
            pair_mask * jax.nn.sigmoid(projected[hidden : 2 * hidden]) * projected[:hidden]
        ).astype(jnp.bfloat16)
        right_proj = (
            pair_mask * jax.nn.sigmoid(projected[3 * hidden :]) * projected[2 * hidden : 3 * hidden]
        ).astype(jnp.bfloat16)
        moved_left = lax.all_to_all(
            left_proj.reshape(hidden, 1, local_rows, local_cols),
            ("row", "ch"),
            split_axis=0,
            concat_axis=1,
            tiled=True,
        )
        moved_right = lax.all_to_all(
            right_proj.reshape(hidden, 1, local_rows, local_cols),
            ("row", "ch"),
            split_axis=0,
            concat_axis=1,
            tiled=True,
        )
        left_chan = arrange_rows(moved_left)
        right_chan = arrange_rows(moved_right)
        if update == 0:
            stacked = right_chan.reshape(per_device, rows_count, 1, local_rows, length)
            result = jnp.einsum(
                "cik,crptk->cirpt",
                left_chan,
                lax.all_gather(stacked, "sub", axis=2, tiled=True),
                preferred_element_type=jnp.float32,
            )
            mixed_hidden = result.reshape(per_device, used_rows, length).astype(jnp.bfloat16)
        else:
            left_stack = left_chan.reshape(per_device, rows_count, 1, local_rows, length)
            right_stack = right_chan.reshape(per_device, rows_count, 1, local_rows, length)
            shard_left = lax.all_gather(left_stack, "sub", axis=2, tiled=True)
            shard_right = lax.all_gather(right_stack, "sub", axis=2, tiled=True)
            span_count = shard_left.shape[2]
            accumulate_shaped = shard_left.reshape(
                per_device, rows_count, span_count, local_rows, rows_count, halves, local_rows
            )
            chosen = lax.dynamic_slice_in_dim(accumulate_shaped, half_index, 1, 5)
            chosen = chosen.reshape(per_device, rows_count, span_count, local_rows, used_rows)
            total = jnp.einsum(
                "crpti,crptj->cij", chosen, shard_right, preferred_element_type=jnp.float32
            )
            mixed_hidden = total.astype(jnp.bfloat16)
        from_shaped = mixed_hidden.reshape(
            per_device, rows_count, local_rows, chan_count, local_cols
        )
        arranged = from_shaped.transpose(0, 1, 3, 2, 4).reshape(
            per_device, rows_count * chan_count, local_rows, local_cols
        )
        returned = lax.all_to_all(arranged, ("row", "ch"), split_axis=1, concat_axis=0, tiled=True)
        mixed_rows = returned.reshape(hidden, local_rows, local_cols)
        gain_vector = output_gain[update]
        weight_rows = output_weight[update]
        mixed_norm = channel_norm(mixed_rows.astype(jnp.float32), gain_vector).astype(jnp.bfloat16)
        update_term = jnp.einsum(
            "dpq,de->epq", mixed_norm, weight_rows, preferred_element_type=jnp.float32
        )
        current = (current.astype(jnp.float32) + gate_value * update_term).astype(jnp.bfloat16)
    return current


def transposed(block):
    return block.astype(F32).T


def moments(ref):
    channels, chunk = ref.shape[0], 16
    total = jnp.zeros(ref.shape[1:], F32)
    for start in range(0, channels, chunk):
        total = total + jnp.sum(ref[start : start + chunk], axis=0)
    average = total / channels
    total = jnp.zeros(ref.shape[1:], F32)
    for start in range(0, channels, chunk):
        total = total + jnp.sum(jnp.square(ref[start : start + chunk] - average), axis=0)
    return average, lax.rsqrt(total / channels + EPS)


def kernel(
    rows_count, halves,
    pair_hbm, mask_hbm, gain_in_hbm, w_proj_hbm, w_gate_hbm, gain_out_hbm, w_out_hbm, out,
    pair, mask, gain_in, w_proj, w_gate, gain_out, w_out,
    current, stage, wt, wg, wo, gcol, normed, gate, pair_mask, slab_stage,
    lsend, rsend, lrecv, rrecv, msend, mrecv,
    in_sem, lsend_sem, lrecv_sem, rsend_sem, rrecv_sem, msend_sem, mrecv_sem,
):
    devices = rows_count * halves
    channels, local_rows, cols = pair.shape
    camp = devices // 2
    plane = 4
    planes = camp // plane
    own = channels // camp // 2
    pack = own * plane
    half_channels = channels // 2
    row, sub = lax.axis_index("row"), lax.axis_index("sub")
    me = row * halves + sub
    my_base = (me // camp) * camp
    far_base = camp - my_base
    my_rank = me % camp
    my_plane = my_rank // plane
    my_seat = my_rank % plane

    fetches = [
        pltpu.make_async_copy(src, dst, in_sem.at[index])
        for index, (src, dst) in enumerate(
            (
                (pair_hbm, pair),
                (w_proj_hbm, w_proj),
                (gain_in_hbm, gain_in),
                (mask_hbm, mask),
                (w_gate_hbm, w_gate),
                (gain_out_hbm, gain_out),
                (w_out_hbm, w_out),
            )
        )
    ]
    for fetch in fetches:
        fetch.start()

    def place(device):
        return {"row": device // halves, "sub": device % halves}

    barrier = pltpu.get_barrier_semaphore()

    def greet(step, carry):
        pl.semaphore_signal(
            barrier, inc=1, device_id=place((me + step) % devices), device_id_type=MESH
        )
        return carry

    lax.fori_loop(1, devices, greet, 0)

    def prepare_projection(update):
        for kind in range(4):
            block = transposed(w_proj[update, :, kind * channels : (kind + 1) * channels])
            wt[update, :, kind * pack : (kind + 1) * pack, :] = block.reshape(
                2 * planes, pack, channels
            ).astype(BF16)
        gcol[2 * update] = jnp.broadcast_to(gain_in[update : update + 1, :], (cols, channels)).T

    def prepare_finish(update):
        wo[update] = transposed(w_out[update]).astype(BF16)
        gcol[2 * update + 1] = jnp.broadcast_to(
            gain_out[update : update + 1, :], (cols, channels)
        ).T

    for fetch in fetches[:4]:
        fetch.wait()
    current[...] = pair[...].astype(F32)
    prepare_projection(0)
    col_mask = mask[...].astype(F32)
    lane = lax.broadcasted_iota(jnp.int32, col_mask.shape, 1)
    for r in range(local_rows):
        mine = jnp.sum(
            jnp.where(lane == me * local_rows + r, col_mask, 0.0), axis=1, keepdims=True
        )
        pair_mask[0:1, r * cols : (r + 1) * cols] = col_mask * mine

    def l_copy(update, half, device, slot):
        return pltpu.make_async_remote_copy(
            src_ref=lsend.at[update, half, device % camp],
            dst_ref=lrecv.at[update, half, slot],
            send_sem=lsend_sem.at[update, half, device % camp],
            recv_sem=lrecv_sem.at[update, half, slot],
            device_id=place(device),
            device_id_type=MESH,
        )

    def r_copy(update, half, device, slot):
        return pltpu.make_async_remote_copy(
            src_ref=rsend.at[update, half, device % camp],
            dst_ref=rrecv.at[update, half, slot],
            send_sem=rsend_sem.at[update, half, device],
            recv_sem=rrecv_sem.at[update, half, slot],
            device_id=place(device),
            device_id_type=MESH,
        )

    def m_copy(update, half, device, slot):
        return pltpu.make_async_remote_copy(
            src_ref=msend.at[update, half, device],
            dst_ref=mrecv.at[update, half, slot],
            send_sem=msend_sem.at[update, half, device],
            recv_sem=mrecv_sem.at[update, half, slot],
            device_id=place(device),
            device_id_type=MESH,
        )

    def normalise(ref, gains):
        average, scale = moments(ref)
        for r in range(local_rows):
            normed[:, r * cols : (r + 1) * cols] = (
                (ref[:, r, :] - average[r : r + 1]) * scale[r : r + 1] * gcol[gains]
            ).astype(BF16)

    for update in range(2):
        normalise(current, 2 * update)

        def project(half, group):
            for part in range(local_rows // 2):
                span = slice(part * 2 * cols, (part + 1) * 2 * cols)
                values = jnp.dot(
                    wt[update, half * planes + group], normed[:, span], preferred_element_type=F32
                )
                masked = pair_mask[0:1, span]
                for side in range(2):
                    base = 2 * side * pack
                    scaled = (
                        masked
                        * jax.nn.sigmoid(values[base + pack : base + 2 * pack])
                        * values[base : base + pack]
                    )
                    for r in range(2):
                        slab_stage[side, :, part * 2 + r, :] = scaled[:, r * cols : (r + 1) * cols]
            for seat in range(plane):
                for side, target in enumerate((lsend, rsend)):
                    target[update, half, group * plane + seat] = (
                        slab_stage[side, seat * own : (seat + 1) * own]
                        .reshape(own * local_rows, cols)
                        .astype(BF16)
                    )

        if update == 0:
            pl.semaphore_wait(barrier, devices - 1)

        r_slot = me if update == 0 else my_rank
        for half in range(2):
            for step in range(1, planes + 1):
                group = (my_plane + step) % planes
                project(half, group)
                for seat in range(plane):
                    rank = group * plane + (my_seat + seat) % plane
                    if update == 0:
                        r_copy(update, half, far_base + rank, r_slot).start()
                    if update == 1 and (step < planes or seat > 0):
                        l_copy(update, half, my_base + rank, my_rank).start()
                        r_copy(update, half, my_base + rank, r_slot).start()
            if update == 0:

                def near_step(step, carry):
                    rank = (my_rank + step) % camp
                    r_copy(update, half, my_base + rank, r_slot).start()
                    l_copy(update, half, my_base + rank, my_rank).start()
                    return carry

                lax.fori_loop(1, camp, near_step, 0)
            lrecv[update, half, my_rank] = lsend[update, half, my_rank]
            rrecv[update, half, r_slot] = rsend[update, half, my_rank]

        if update == 0:
            for fetch in fetches[4:]:
                fetch.wait()
            for later in range(2):
                wg[later] = transposed(w_gate[later]).astype(BF16)
        for part in range(local_rows // 2):
            span = slice(part * 2 * cols, (part + 1) * 2 * cols)
            gate[:, span] = jax.nn.sigmoid(
                jnp.dot(wg[update], normed[:, span], preferred_element_type=F32)
            )
        if update == 0:
            prepare_finish(0)
            prepare_projection(1)
            prepare_finish(1)

        contract = ((1,), (1,)) if update == 0 else ((0,), (0,))
        sources = devices if update == 0 else camp
        targets = camp if update == 0 else devices
        for half in range(2):

            def near_arrived(step, carry):
                rank = (my_rank + step) % camp
                l_copy(update, half, my_base + rank, rank).wait_recv()
                slot = my_base + rank if update == 0 else rank
                r_copy(update, half, my_base + rank, slot).wait_recv()
                return carry

            lax.fori_loop(1, camp, near_arrived, 0)
            if update == 0:

                def far_arrived(step, carry):
                    device = far_base + (my_rank + step) % camp
                    r_copy(update, half, device, device).wait_recv()
                    return carry

                lax.fori_loop(0, camp, far_arrived, 0)
            for couple in range(own // 2):
                span = slice(couple * 2 * local_rows, (couple + 1) * 2 * local_rows)
                lefts = lrecv[update, half, :, span, :].astype(F32)
                lefts = lefts.reshape(camp, 2, local_rows, cols)
                rights = rrecv[update, half, :sources, span, :].astype(F32)
                rights = rights.reshape(sources, 2, local_rows, cols)
                products = []
                for c in range(2):
                    product = lax.dot_general(
                        lefts[:, c].reshape(camp * local_rows, cols).astype(BF16),
                        rights[:, c].reshape(sources * local_rows, cols).astype(BF16),
                        (contract, ((), ())),
                        preferred_element_type=F32,
                    )
                    products.append(product.reshape(targets, 1, local_rows, cols))
                block = (
                    jnp.concatenate(products, axis=1)
                    .reshape(targets, 2 * local_rows, cols)
                    .astype(BF16)
                )
                if update == 0:
                    msend[update, half, pl.ds(my_base, camp), span, :] = block
                else:
                    msend[update, half, :, span, :] = block

            if update == 1:

                def m_far(step, carry):
                    rank = (my_rank + step) % camp
                    m_copy(update, half, far_base + rank, camp + my_rank).start()
                    return carry

                lax.fori_loop(0, camp, m_far, 0)

            def m_near(step, carry):
                rank = (my_rank + step) % camp
                m_copy(update, half, my_base + rank, my_rank).start()
                return carry

            lax.fori_loop(1, camp, m_near, 0)
            mrecv[update, half, my_rank] = msend[update, half, me]

        for half in range(2):

            def m_arrived(step, carry):
                rank = (my_rank + step) % camp
                m_copy(update, half, my_base + rank, rank).wait_recv()
                return carry

            lax.fori_loop(1, camp, m_arrived, 0)
            mixed = mrecv[update, half, :camp].astype(F32)
            if update == 1:

                def m_far_arrived(step, carry):
                    rank = (my_rank + step) % camp
                    m_copy(update, half, far_base + rank, camp + rank).wait_recv()
                    return carry

                lax.fori_loop(0, camp, m_far_arrived, 0)
                mixed = mixed + mrecv[update, half, camp:].astype(F32)
            stage[half * half_channels : (half + 1) * half_channels] = mixed.reshape(
                half_channels, local_rows, cols
            )

        normalise(stage, 2 * update + 1)
        for part in range(local_rows // 2):
            span = slice(part * 2 * cols, (part + 1) * 2 * cols)
            term = gate[:, span] * jnp.dot(wo[update], normed[:, span], preferred_element_type=F32)
            for r in range(2):
                stage[:, part * 2 + r, :] = term[:, r * cols : (r + 1) * cols]
        fresh = (current[...] + stage[...]).astype(BF16)
        if update == 0:
            current[...] = fresh.astype(F32)
        else:
            out[...] = fresh

    for update in range(2):
        for half in range(2):

            def near_sent(step, carry):
                device = my_base + (my_rank + step) % camp
                l_copy(update, half, device, my_rank).wait_send()
                r_copy(update, half, device, my_rank).wait_send()
                m_copy(update, half, device, my_rank).wait_send()
                return carry

            lax.fori_loop(1, camp, near_sent, 0)

            def far_sent(step, carry):
                device = far_base + (my_rank + step) % camp
                if update == 0:
                    r_copy(update, half, device, me).wait_send()
                else:
                    m_copy(update, half, device, camp + my_rank).wait_send()
                return carry

            lax.fori_loop(0, camp, far_sent, 0)


def fused_body(rows_count, halves, pair, mask, gain_in, w_proj, w_gate, gain_out, w_out):
    channels, local_rows, cols = pair.shape
    devices = rows_count * halves
    camp = devices // 2
    own = channels // camp // 2
    slab = own * local_rows
    pack = own * 4
    wide = local_rows * cols
    operands = (pair, mask.reshape(1, -1), gain_in, w_proj, w_gate, gain_out, w_out)
    vmem = pl.BlockSpec(memory_space=pltpu.VMEM)
    hbm = pl.BlockSpec(memory_space=pltpu.HBM)
    return pl.pallas_call(
        functools.partial(kernel, rows_count, halves),
        out_shape=jax.ShapeDtypeStruct(pair.shape, BF16),
        in_specs=[hbm] * 7,
        out_specs=vmem,
        scratch_shapes=[pltpu.VMEM(each.shape, each.dtype) for each in operands]
        + [
            pltpu.VMEM(pair.shape, F32),
            pltpu.VMEM(pair.shape, F32),
            pltpu.VMEM((2, camp // 2, 4 * pack, channels), BF16),
            pltpu.VMEM((2, channels, channels), BF16),
            pltpu.VMEM((2, channels, channels), BF16),
            pltpu.VMEM((4, channels, cols), F32),
            pltpu.VMEM((channels, wide), BF16),
            pltpu.VMEM((channels, wide), F32),
            pltpu.VMEM((8, wide), F32),
            pltpu.VMEM((2, pack, local_rows, cols), F32),
            pltpu.VMEM((2, 2, camp, slab, cols), BF16),
            pltpu.VMEM((2, 2, camp, slab, cols), BF16),
            pltpu.VMEM((2, 2, camp, slab, cols), BF16),
            pltpu.VMEM((2, 2, devices, slab, cols), BF16),
            pltpu.VMEM((2, 2, devices, slab, cols), BF16),
            pltpu.VMEM((2, 2, devices, slab, cols), BF16),
            pltpu.SemaphoreType.DMA((7,)),
            pltpu.SemaphoreType.DMA((2, 2, camp)),
            pltpu.SemaphoreType.DMA((2, 2, camp)),
            pltpu.SemaphoreType.DMA((2, 2, devices)),
            pltpu.SemaphoreType.DMA((2, 2, devices)),
            pltpu.SemaphoreType.DMA((2, 2, devices)),
            pltpu.SemaphoreType.DMA((2, 2, devices)),
        ],
        compiler_params=pltpu.CompilerParams(
            collective_id=0, has_side_effects=True, vmem_limit_bytes=60 * 2**20
        ),
    )(*operands)


def body(*args):
    rows_count, halves = lax.axis_size("row"), lax.axis_size("sub")
    channels, local_rows, cols = args[0].shape
    hidden = args[6].shape[1]
    devices = rows_count * halves
    fits = (
        lax.axis_size("ch") == 1
        and hidden == channels
        and devices % 8 == 0
        and local_rows == 8
        and cols == devices * local_rows
        and channels == devices * 8
        and cols % 128 == 0
    )
    if fits:
        return fused_body(rows_count, halves, *args)
    return split_body(*args)


def solution(mesh):
    placed = (P(None, ("grp", "row", "sub"), "ch"), P("grp"), P(), P(), P(), P(), P())
    return jax.shard_map(
        body,
        mesh=mesh,
        in_specs=placed,
        out_specs=P(None, ("grp", "row", "sub"), "ch"),
        check_vma=False,
    )
```
